32 devices in a mesh: parts: 2 (over y), grp: 4 (over z), mem: 4 (over x, core).
Axes of the slice: x: 2, y: 2, z: 4, core: 2. Of those that a mesh axis runs over, the one named last changes fastest.
Arguments:
- points: bfloat16 [6144, 1024], P(('parts', 'grp', 'mem')), parts along dimension 0, may hold values from -6 to 6
- cluster: int32 [6144, 1], P(('parts', 'grp', 'mem')), parts along dimension 0, may hold values from 0 to 3, as said below
- assign: int32 [6144], P(('parts', 'grp', 'mem')), parts along dimension 0, may hold values from 0 to 4095
- centroids: bfloat16 [8, 4096, 1024], P(('parts', 'grp'), 'mem'), parts along dimension 0, may hold values from -6 to 6
- prior_counts: int32 [8, 4096], P(('parts', 'grp'), 'mem'), parts along dimension 0, may hold values from 1 to 64
Outputs:
- new_centroids: bfloat16 [8, 4096, 1024], P(('parts', 'grp'), 'mem'), parts along dimension 0
- point_cost: float32 [6144], P(('parts', 'grp', 'mem')), parts along dimension 0
The draws below stay inside these ranges and needn't reach their ends.
There are 2 independent parts, one for each index of `parts`. The reference program is written for one: setup_inputs(seed, part) draws one part's arguments, and reference() takes and returns one part's arrays. A program takes and returns all parts, laid end to end along the dimension named above; each array names one. Nothing has to cross between parts.
Inputs may be any that keep to these rules, and one draw needn't show every extreme that they name: No device holds more than 96 points of one first-level cluster; some device holds exactly 96. The first-level clusters differ in size about tenfold.
All inputs are finite; a program needn't handle non-finite values.
Results may differ from the reference program's by a relative error of at most 0.001.
Values may be sent and summed in bfloat16 or wider, within the bound.
A program may use at most 64 MiB of HBM per device.

```python
import jax
import jax.numpy as jnp
from jax import lax

D = 1024
K = 4096
TOK = 192
CLUSTERS = 4
CAP = 96
ROWS = 3072
N_GRP = 4
N_MEM = 4


def draw_cluster(key, part):
    key = jax.random.fold_in(key, 11)
    groups = N_GRP
    half = groups // 2
    slot_cap = 2 * TOK // groups
    lowest = max(1, slot_cap // 10)
    blocks = ROWS // TOK
    ranks = jnp.arange(half, dtype=jnp.int32)
    light = lowest + ranks * (slot_cap // 2 - lowest) // half
    light_rows = jnp.broadcast_to(light[None, :], (blocks, half))
    first = (jnp.arange(blocks, dtype=jnp.int32) == 0)[:, None] & (ranks == 0)[None, :]
    light_rows = jnp.where(first, 0, light_rows).astype(jnp.int32)
    heavy_rows = (slot_cap - light_rows)[:, ::-1]
    rank_counts = jnp.concatenate([light_rows, heavy_rows], axis=1).astype(jnp.int32)
    ends = jnp.cumsum(rank_counts, axis=1).astype(jnp.int32)
    places = jnp.arange(TOK, dtype=jnp.int32)
    rank_of = jnp.sum((places[None, :, None] >= ends[:, None, :]).astype(jnp.int32), axis=2).astype(jnp.int32)
    order = jax.random.permutation(jax.random.fold_in(key, 1), groups).astype(jnp.int32)
    labels = order[rank_of]
    block_keys = jax.random.split(jax.random.fold_in(key, 2), blocks)
    shuffles = jax.vmap(lambda one_key: jax.random.permutation(one_key, TOK))(block_keys).astype(jnp.int32)
    labels = jnp.take_along_axis(labels, shuffles, axis=1)
    return labels.reshape(ROWS, 1).astype(jnp.int32)


def place_ends(result, stream_key, least, high):
    place = [jax.random.randint(jax.random.fold_in(stream_key, axis), (), 0, length) for axis, length in enumerate(result.shape)]
    longest = result.shape.index(max(result.shape))
    neighbour = place[:longest] + [(place[longest] + 1) % result.shape[longest]] + place[longest + 1:]
    return result.at[tuple(place)].set(least).at[tuple(neighbour)].set(high)


def levels(own_key, shape, shards, smallest, largest):
    def one(axis_at, shards_of):
        steps = jax.random.uniform(jax.random.fold_in(jax.random.fold_in(own_key, 6), axis_at), (shards_of,), jnp.float32, smallest / len(shards), largest / len(shards))
        return jnp.repeat(jnp.exp(steps), shape[axis_at] // shards_of).reshape((-1,) + (1,) * (len(shape) - axis_at - 1))

    gain = one(*shards[0])
    for cut in shards[1:]:
        gain = gain * one(*cut)
    return gain


def bell_draw(key, extent, scale, limit, cuts=(), kind=jnp.bfloat16):
    array = jax.random.normal(key, extent, jnp.float32) * scale
    if len(cuts) > 0:
        array = levels(key, extent, cuts, -0.22, 0.18) * array
    return jnp.clip(array, min=-limit, max=limit).astype(kind)


def setup_inputs(seed: int = 0, part: int = 0) -> dict:
    seeds = jax.random.split(jax.random.key(seed), 6)
    own_keys = jax.random.split(jax.random.fold_in(seeds[5], part), 6)
    return {
        "points": bell_draw(own_keys[0], (ROWS, D), 1.0, 6.0, ((0, 16),)),
        "cluster": draw_cluster(jax.random.fold_in(jax.random.fold_in(seeds[5], part), 71), part),
        "assign": place_ends(jax.random.randint(own_keys[2], (ROWS,), 0, K), jax.random.fold_in(own_keys[2], 1), 0, K - 1).astype(jnp.int32),
        "centroids": bell_draw(own_keys[3], (CLUSTERS, K, D), 1.0, 6.0, ((0, 4), (1, 4))),
        "prior_counts": place_ends(jax.random.randint(own_keys[4], (CLUSTERS, K), 1, 65), jax.random.fold_in(own_keys[4], 1), 1, 64).astype(jnp.int32),
    }


def reference(points, cluster, assign, centroids, prior_counts):
    clusters, width, feats = centroids.shape
    total_rows = points.shape[0]
    cluster_ids = cluster[:, 0].astype(jnp.int32)
    codes = cluster_ids * width + assign.astype(jnp.int32)
    values = points.astype(jnp.float32)
    sums = jax.ops.segment_sum(values, codes, num_segments=clusters * width)
    counts = jax.ops.segment_sum(jnp.ones(codes.shape, jnp.float32), codes, num_segments=clusters * width)
    weight = prior_counts.reshape(-1).astype(jnp.float32)
    old_values = centroids.reshape(-1, feats).astype(jnp.float32)
    fresh = ((weight[:, None] * old_values + sums) / (weight + counts)[:, None]).astype(jnp.bfloat16)
    fresh = fresh.reshape(clusters, width, feats)
    row_sq = jnp.sum(values * values, axis=1)
    slot_total = N_GRP * N_MEM * CAP

    def one_cluster(index):
        chosen = jnp.nonzero(cluster_ids == index, size=slot_total, fill_value=total_rows)[0].astype(jnp.int32)
        rows = jnp.take(points, chosen, axis=0, mode="clip")
        centre = lax.dynamic_index_in_dim(fresh, index, 0, keepdims=False)
        centre_f = centre.astype(jnp.float32)
        centre_sq = jnp.sum(centre_f * centre_f, axis=1)
        cross = lax.dot_general(rows, centre, (((1,), (1,)), ((), ())), preferred_element_type=jnp.float32)
        return chosen, jnp.min(centre_sq[None, :] - 2.0 * cross, axis=1)

    chosen, best = lax.map(one_cluster, jnp.arange(clusters, dtype=jnp.int32))
    nearest = jnp.zeros((total_rows + 1,), jnp.float32).at[chosen.reshape(-1)].set(best.reshape(-1))[:total_rows]
    point_cost = (row_sq + nearest) / feats
    return fresh, point_cost
```

```python
import functools

import jax
import jax.numpy as jnp
from jax import lax
from jax.experimental import pallas as pl
from jax.experimental.pallas import tpu as pltpu
from jax.sharding import PartitionSpec as P

MESH = pl.DeviceIdType.MESH
F32 = jnp.float32
BF16 = jnp.bfloat16


def round_up(value, unit):
    return (value + unit - 1) // unit * unit


def kernel(
    groups, mems, cap, cuts, points_ref, cluster_ref, assign_ref, prior_ref, old_ref,
    fresh_ref, cost_ref,
    send_rows, rows, ids_out, ids_in, low_out, low_in, old, fresh, total, counted,
    z_send, x_send, core_send, row_recv, ids_send, ids_recv, low_send, low_recv, old_sem, fresh_sem,
):
    tok, feats = points_ref.shape
    width = old.shape[0]
    everyone = groups * mems
    xs = mems // 2
    cut = cap // cuts
    tile = min(256, width)
    tiles = width // tile
    g = lax.axis_index("grp")
    m = lax.axis_index("mem")
    x = m // 2
    core = m % 2
    near = m + 1 - 2 * core
    me = g * mems + m

    load_old = pltpu.make_async_copy(old_ref.at[0], old, old_sem)
    load_old.start()

    def where_is(flat):
        return {"grp": flat // mems, "mem": flat % mems}

    def each_other(body):
        def one(step, carry):
            body(lax.rem(me + step, everyone))
            return carry

        lax.fori_loop(1, everyone, one, 0)

    barrier = pltpu.get_barrier_semaphore()
    each_other(
        lambda flat: pl.semaphore_signal(
            barrier, inc=1, device_id=where_is(flat), device_id_type=MESH
        )
    )

    member = cluster_ref[...] == lax.broadcasted_iota(jnp.int32, (groups, tok), 0)
    before = lax.broadcasted_iota(jnp.int32, (tok, tok), 0) < lax.broadcasted_iota(
        jnp.int32, (tok, tok), 1
    )
    rank = jnp.dot(
        member.astype(F32).astype(BF16), before.astype(F32).astype(BF16),
        preferred_element_type=F32,
    )
    first_slot = (lax.broadcasted_iota(jnp.int32, (groups, tok), 0) * cap).astype(F32)
    target = jnp.sum(jnp.where(member, rank + first_slot, 0.0), axis=0, keepdims=True).astype(
        jnp.int32
    )
    assign = assign_ref[...]
    digit = lax.broadcasted_iota(jnp.int32, (8, tok), 0)
    digits = jnp.where(
        digit == 0, assign // 256, jnp.where(digit == 1, assign % 256, 1)
    ).astype(F32).astype(BF16)
    points = points_ref[...]

    def placed(c):
        slot = lax.broadcasted_iota(jnp.int32, (cap, tok), 0) + c * cap
        return slot == target

    for c in range(groups):
        place = placed(c).astype(F32).astype(BF16)
        send_rows[c] = jnp.dot(place, points, preferred_element_type=F32).astype(BF16)
        found = lax.dot_general(
            digits, place, (((1,), (1,)), ((), ())), preferred_element_type=F32
        ).astype(jnp.int32)
        code = jnp.where(found[2:3] > 0, found[0:1] * 256 + found[1:2], -1)
        ids_out[c, :, 0:cap] = jnp.broadcast_to(code, (8, cap))

    pl.semaphore_wait(barrier, everyone - 1)

    def copy(src, dst, send, recv, where):
        return pltpu.make_async_remote_copy(
            src_ref=src, dst_ref=dst, send_sem=send, recv_sem=recv, device_id=where,
            device_id_type=MESH,
        )

    def part(i):
        return pl.ds(i * cut, cut)

    def z_copy(c, i):
        return copy(
            send_rows.at[c, part(i)], rows.at[g, m, part(i)], z_send.at[c, i],
            row_recv.at[g, m, i], {"grp": c},
        )

    def x_copy(j, s, i):
        there = lax.rem(x + s, xs) * 2 + core
        spot = rows.at[j, m, part(i)]
        return copy(spot, spot, x_send.at[j, s - 1, i], row_recv.at[j, m, i], {"mem": there})

    def core_copy(j, mm, i):
        spot = rows.at[j, mm, part(i)]
        return copy(spot, spot, core_send.at[j, mm, i], row_recv.at[j, mm, i], {"mem": near})

    def wait_rows(j, mm, i):
        core_copy(j, mm, i).wait_recv()

    def ids_copy(flat):
        return copy(
            ids_out.at[flat // mems], ids_in.at[me], ids_send.at[flat], ids_recv.at[me],
            where_is(flat),
        )

    def low_copy(flat):
        return copy(
            low_out.at[flat], low_in.at[me], low_send.at[flat], low_recv.at[me], where_is(flat)
        )

    def ids_arrival(flat):
        copy(
            ids_out.at[flat // mems], ids_in.at[flat], ids_send.at[flat], ids_recv.at[flat],
            where_is(flat),
        ).wait()

    half = groups // 2
    order = [half] + [s for d in range(1, half) for s in (half - d, half + d)] if groups > 1 else []
    for i in range(cuts):
        for s in order:
            z_copy(lax.rem(g + s, groups), i).start()
    rows[g, m] = send_rows[g]
    ids_in[me] = ids_out[g]

    def forward_own(j, i):
        for s in range(1, xs):
            x_copy(j, s, i).start()
        core_copy(j, m, i).start()

    for i in range(cuts):
        forward_own(g, i)
    each_other(lambda flat: ids_copy(flat).start())

    prior = jnp.broadcast_to(prior_ref[...].astype(F32), (128, width)).T
    counted[...] = prior
    load_old.wait()

    def weigh(t, carry):
        at = pl.ds(pl.multiple_of(t * tile, tile), tile)
        total[at, :] = old[at, :].astype(F32) * counted[at, 0:1]
        return carry

    lax.fori_loop(0, tiles, weigh, 0)
    first_code = m * width

    def chunk_codes(j):
        return jnp.concatenate([ids_in[j * mems + mm][0:1, 0:cap] for mm in range(mems)], axis=1)

    def onehot_tile(codes, t):
        code = lax.broadcasted_iota(jnp.int32, (tile, mems * cap), 0) + (first_code + t * tile)
        return (code == codes).astype(F32).astype(BF16)

    ones = jnp.ones((mems * cap, 128), BF16)

    def add_chunk(j):
        codes = chunk_codes(j)
        block = rows[j].reshape(mems * cap, feats)

        def one(t, carry):
            at = pl.ds(pl.multiple_of(t * tile, tile), tile)
            onehot = onehot_tile(codes, t)
            total[at, :] += jnp.dot(onehot, block, preferred_element_type=F32)
            counted[at, :] += jnp.dot(onehot, ones, preferred_element_type=F32)
            return carry

        lax.fori_loop(0, tiles, one, 0)

    def x_arrivals(j, i):
        for s in range(1, xs):
            mm = lax.rem(x + s, xs) * 2 + core
            wait_rows(j, mm, i)
            core_copy(j, mm, i).start()

    def core_arrivals(j):
        for i in range(cuts):
            for s in range(xs):
                wait_rows(j, lax.rem(x + s, xs) * 2 + 1 - core, i)

    sources = [g] + [lax.rem(g + groups - s, groups) for s in order]
    for step in range(1, groups + 2):
        for i in range(cuts):
            if step < groups:
                wait_rows(sources[step], m, i)
                forward_own(sources[step], i)
            if step <= groups:
                x_arrivals(sources[step - 1], i)
        if step == 1:
            each_other(ids_arrival)
        else:
            core_arrivals(sources[step - 2])
            add_chunk(sources[step - 2])

    def store_fresh(t):
        at = pl.ds(pl.multiple_of(t * tile, tile), tile)
        return pltpu.make_async_copy(fresh.at[at, :], fresh_ref.at[0, at, :], fresh_sem.at[t])

    every = groups * mems * cap

    def finish(t, low):
        at = pl.ds(pl.multiple_of(t * tile, tile), tile)
        new = (total[at, :] * (1.0 / counted[at, 0:1])).astype(BF16)
        fresh[at, :] = new
        store_fresh(t).start()
        new_f = new.astype(F32)
        square = jnp.sum(new_f * new_f, axis=1, keepdims=True)
        cross = lax.dot_general(
            new, rows[...].reshape(every, feats), (((1,), (1,)), ((), ())),
            preferred_element_type=F32,
        )
        return jnp.minimum(low, jnp.min(square - 2.0 * cross, axis=0, keepdims=True))

    low = lax.fori_loop(0, tiles, finish, jnp.full((1, every), jnp.inf, F32))
    for flat in range(everyone):
        low_out[flat, :, 0:cap] = jnp.broadcast_to(
            low[:, flat * cap:(flat + 1) * cap], (8, cap)
        )
    low_in[me] = low_out[me]
    each_other(lambda flat: low_copy(flat).start())

    values = points_ref[...].astype(F32)
    row_sq = jnp.sum(values * values, axis=1, keepdims=True)
    row_sq = jnp.broadcast_to(row_sq, (tok, 128)).T[0:1]

    for i in range(cuts):
        for s in order:
            z_copy(lax.rem(g + s, groups), i).wait_send()
        for j in sources:
            for s in range(1, xs):
                x_copy(j, s, i).wait_send()
                core_copy(j, lax.rem(x + s, xs) * 2 + core, i).wait_send()
            core_copy(j, m, i).wait_send()
    each_other(lambda flat: low_copy(flat).wait_send())

    def low_arrival(flat):
        copy(
            low_out.at[flat], low_in.at[flat], low_send.at[flat], low_recv.at[flat],
            where_is(flat),
        ).wait_recv()

    each_other(low_arrival)
    best = jnp.zeros((1, tok), F32)
    for c in range(groups):
        lowest = low_in[c * mems]
        for mm in range(1, mems):
            lowest = jnp.minimum(lowest, low_in[c * mems + mm])
        column = jnp.broadcast_to(lowest[0:1], (128, 128)).T[0:cap, 0:1]
        best += jnp.sum(jnp.where(placed(c), column, 0.0), axis=0, keepdims=True)
    cost_ref[...] = (row_sq + best) / feats

    def stored(t, carry):
        store_fresh(t).wait()
        return carry

    lax.fori_loop(0, tiles, stored, 0)


def local(points, cluster, assign, centroids, prior_counts):
    groups = lax.axis_size("grp")
    mems = lax.axis_size("mem")
    tok, feats = points.shape
    width = centroids.shape[1]
    cap = round_up(2 * tok // groups, 16)
    cuts = 2 if cap % 32 == 0 else 1
    everyone = groups * mems
    xs = mems // 2
    tiles = width // min(256, width)
    dma = pltpu.SemaphoreType.DMA
    vmem = pl.BlockSpec(memory_space=pltpu.VMEM)
    anywhere = pl.BlockSpec(memory_space=pl.ANY)
    fresh, cost = pl.pallas_call(
        functools.partial(kernel, groups, mems, cap, cuts),
        out_shape=(
            jax.ShapeDtypeStruct(centroids.shape, BF16),
            jax.ShapeDtypeStruct((1, tok), F32),
        ),
        in_specs=[vmem, vmem, vmem, vmem, anywhere],
        out_specs=(anywhere, vmem),
        scratch_shapes=[
            pltpu.VMEM((groups, cap, feats), BF16),
            pltpu.VMEM((groups, mems, cap, feats), BF16),
            pltpu.VMEM((groups, 8, 128), jnp.int32),
            pltpu.VMEM((everyone, 8, 128), jnp.int32),
            pltpu.VMEM((everyone, 8, 128), F32),
            pltpu.VMEM((everyone, 8, 128), F32),
            pltpu.VMEM((width, feats), BF16),
            pltpu.VMEM((width, feats), BF16),
            pltpu.VMEM((width, feats), F32),
            pltpu.VMEM((width, 128), F32),
            dma((groups, cuts)),
            dma((groups, max(1, xs - 1), cuts)),
            dma((groups, mems, cuts)),
            dma((groups, mems, cuts)),
            dma((everyone,)),
            dma((everyone,)),
            dma((everyone,)),
            dma((everyone,)),
            dma,
            dma((tiles,)),
        ],
        compiler_params=pltpu.CompilerParams(
            collective_id=0, has_side_effects=True, vmem_limit_bytes=56 * 1024 * 1024
        ),
        cost_estimate=pl.CostEstimate(
            flops=4 * everyone * cap * width * feats,
            bytes_accessed=4 * width * feats + 2 * tok * feats,
            transcendentals=0,
        ),
    )(points, cluster.reshape(1, tok), assign.reshape(1, tok), prior_counts, centroids)
    return fresh, cost.reshape(tok)


def solution(mesh):
    placed = (
        P(("parts", "grp", "mem"), None),
        P(("parts", "grp", "mem"), None),
        P(("parts", "grp", "mem")),
        P(("parts", "grp"), "mem", None),
        P(("parts", "grp"), "mem"),
    )
    return jax.shard_map(
        local,
        mesh=mesh,
        in_specs=placed,
        out_specs=(P(("parts", "grp"), "mem", None), P(("parts", "grp", "mem"))),
        check_vma=False,
    )
```

```python
import functools

import jax
import jax.numpy as jnp
from jax import lax
from jax.experimental import pallas as pl
from jax.experimental.pallas import tpu as pltpu
from jax.sharding import PartitionSpec as P

MESH = pl.DeviceIdType.MESH
F32 = jnp.float32
BF16 = jnp.bfloat16
LAG = 1


def round_up(value, unit):
    return (value + unit - 1) // unit * unit


def kernel(
    groups, mems, cut, points_ref, cluster_ref, assign_ref, prior_ref, old_ref,
    fresh_ref, cost_ref,
    send_rows, rows, ids_out, ids_in, low_out, low_in, old, total, counted, lowest,
    z_send, x_send, core_send, row_recv, ids_send, ids_recv, low_send, low_recv, old_sem,
):
    tok, feats = points_ref.shape
    width = old.shape[0]
    everyone = groups * mems
    xs = mems // 2
    cuts = rows.shape[0]
    cap = cuts * cut
    lanes = mems * cut
    tile = min(256, width)
    tiles = width // tile
    g = lax.axis_index("grp")
    m = lax.axis_index("mem")
    x = m // 2
    core = m % 2
    near = m + 1 - 2 * core
    me = g * mems + m

    load_old = pltpu.make_async_copy(old_ref.at[0], old, old_sem)
    load_old.start()

    def where_is(flat):
        return {"grp": flat // mems, "mem": flat % mems}

    def each_other(body):
        def one(step, carry):
            body(lax.rem(me + step, everyone))
            return carry

        lax.fori_loop(1, everyone, one, 0, unroll=everyone <= 16)

    barrier = pltpu.get_barrier_semaphore()
    each_other(
        lambda flat: pl.semaphore_signal(
            barrier, inc=1, device_id=where_is(flat), device_id_type=MESH
        )
    )

    member = cluster_ref[...] == lax.broadcasted_iota(jnp.int32, (groups, tok), 0)
    before = lax.broadcasted_iota(jnp.int32, (tok, tok), 0) < lax.broadcasted_iota(
        jnp.int32, (tok, tok), 1
    )
    rank = jnp.dot(
        member.astype(F32).astype(BF16), before.astype(F32).astype(BF16),
        preferred_element_type=F32,
    )
    first_slot = (lax.broadcasted_iota(jnp.int32, (groups, tok), 0) * cap).astype(F32)
    target = jnp.sum(jnp.where(member, rank + first_slot, 0.0), axis=0, keepdims=True).astype(
        jnp.int32
    )

    points = points_ref[...]
    for c in range(groups):
        slot = lax.broadcasted_iota(jnp.int32, (cap, tok), 0) + c * cap
        place = (slot == target).astype(F32).astype(BF16)
        send_rows[c] = jnp.dot(place, points, preferred_element_type=F32).astype(BF16)

    lane = lax.broadcasted_iota(jnp.int32, (lanes, tok), 0) - m * cut
    own_lane = jnp.where((lane >= 0) & (lane < cut), lane, -groups * cap)

    def spread(c, i):
        return own_lane + (c * cap + i * cut) == target

    pl.semaphore_wait(barrier, everyone - 1)

    def copy(src, dst, send, recv, where):
        return pltpu.make_async_remote_copy(
            src_ref=src, dst_ref=dst, send_sem=send, recv_sem=recv, device_id=where,
            device_id_type=MESH,
        )

    def z_copy(c, i):
        return copy(
            send_rows.at[c, pl.ds(i * cut, cut)], rows.at[i, g, m], z_send.at[c, i],
            row_recv.at[g, m, i], {"grp": c},
        )

    def x_copy(j, s, i):
        there = lax.rem(x + s, xs) * 2 + core
        spot = rows.at[i, j, m]
        return copy(spot, spot, x_send.at[j, s - 1, i], row_recv.at[j, m, i], {"mem": there})

    def core_copy(j, mm, i):
        spot = rows.at[i, j, mm]
        return copy(spot, spot, core_send.at[j, mm, i], row_recv.at[j, mm, i], {"mem": near})

    def wait_rows(j, mm, i):
        core_copy(j, mm, i).wait_recv()

    def ids_copy(flat):
        return copy(
            ids_out.at[flat // mems], ids_in.at[me], ids_send.at[flat], ids_recv.at[me],
            where_is(flat),
        )

    def ids_arrival(flat):
        copy(
            ids_out.at[flat // mems], ids_in.at[flat], ids_send.at[flat], ids_recv.at[flat],
            where_is(flat),
        ).wait()

    def low_copy(flat):
        return copy(
            low_out.at[flat // mems], low_in.at[me], low_send.at[flat], low_recv.at[me],
            where_is(flat),
        )

    def low_arrival(flat):
        copy(
            low_out.at[flat // mems], low_in.at[flat], low_send.at[flat], low_recv.at[flat],
            where_is(flat),
        ).wait()

    half = groups // 2
    order = [half] + [s for d in range(1, half) for s in (half - d, half + d)]
    for i in range(cuts):
        for s in order:
            z_copy(lax.rem(g + s, groups), i).start()

    def forward_own(j, i):
        for s in range(1, xs):
            x_copy(j, s, i).start()
        core_copy(j, m, i).start()

    for i in range(cuts):
        rows[i, g, m] = send_rows[g, i * cut:(i + 1) * cut]
    for i in range(cuts):
        forward_own(g, i)

    assign = assign_ref[...]
    digit = lax.broadcasted_iota(jnp.int32, (8, tok), 0)
    digits = jnp.where(
        digit == 0, assign // 256, jnp.where(digit == 1, assign % 256, 1)
    ).astype(F32).astype(BF16)
    for c in range(groups):
        for i in range(cuts):
            found = lax.dot_general(
                digits, spread(c, i).astype(F32).astype(BF16), (((1,), (1,)), ((), ())),
                preferred_element_type=F32,
            ).astype(jnp.int32)
            ids_out[c, i:i + 1, :] = jnp.where(
                found[2:3] > 0, found[0:1] * 256 + found[1:2], -1
            )
    each_other(lambda flat: ids_copy(flat).start())
    ids_in[me] = ids_out[g]

    counted[...] = jnp.broadcast_to(prior_ref[...].astype(F32), (128, width)).T
    load_old.wait()

    def weigh(t, carry):
        at = pl.ds(pl.multiple_of(t * tile, tile), tile)
        total[at, :] = old[at, :].astype(F32) * counted[at, 0:1]
        return carry

    lax.fori_loop(0, tiles, weigh, 0)
    values = points.astype(F32)
    row_sq = jnp.sum(values * values, axis=1, keepdims=True)
    row_sq = jnp.broadcast_to(row_sq, (tok, 128)).T[0:1]
    each_other(ids_arrival)

    chunk = groups * lanes
    first_code = m * width
    ones = jnp.ones((chunk, 128), BF16)

    def chunk_codes(i):
        found = []
        for j in range(groups):
            codes = ids_in[j * mems, i:i + 1, :]
            for mm in range(1, mems):
                codes = jnp.maximum(codes, ids_in[j * mems + mm, i:i + 1, :])
            found.append(codes)
        return jnp.concatenate(found, axis=1)

    def summed(codes, i, t):
        code = lax.broadcasted_iota(jnp.int32, (tile, chunk), 0) + (first_code + t * tile)
        onehot = (code == codes).astype(F32).astype(BF16)
        sums = jnp.dot(onehot, rows[i].reshape(chunk, feats), preferred_element_type=F32)
        return sums, jnp.dot(onehot, ones, preferred_element_type=F32)

    def add_chunk(i):
        codes = chunk_codes(i)

        def one(t, carry):
            at = pl.ds(pl.multiple_of(t * tile, tile), tile)
            sums, counts = summed(codes, i, t)
            total[at, :] += sums
            counted[at, :] += counts
            return carry

        lax.fori_loop(0, tiles, one, 0)

    def x_arrivals(j, i):
        for s in range(1, xs):
            mm = lax.rem(x + s, xs) * 2 + core
            wait_rows(j, mm, i)
            core_copy(j, mm, i).start()

    def core_arrivals(i):
        for j in sources:
            for s in range(xs):
                wait_rows(j, lax.rem(x + s, xs) * 2 + 1 - core, i)

    sources = [g] + [lax.rem(g + groups - s, groups) for s in order]
    ticks = [(i, step) for i in range(cuts) for step in range(1, groups)]
    last = len(ticks) - 1
    for n, (i, step) in enumerate(ticks):
        wait_rows(sources[step], m, i)
        forward_own(sources[step], i)
        if n < cuts:
            x_arrivals(g, n)
        if n >= LAG:
            before_i, before_step = ticks[n - LAG]
            x_arrivals(sources[before_step], before_i)
        if step == groups - 1 and 1 <= i:
            core_arrivals(i - 1)
            add_chunk(i - 1)
    for n in range(last + 1, cuts):
        x_arrivals(g, n)
    for before_i, before_step in ticks[last + 1 - LAG:]:
        x_arrivals(sources[before_step], before_i)
    core_arrivals(cuts - 1)

    codes = chunk_codes(cuts - 1)
    lowest[...] = jnp.full(lowest.shape, jnp.inf, F32)

    def finish(t, carry):
        at = pl.ds(pl.multiple_of(t * tile, tile), tile)
        sums, counts = summed(codes, cuts - 1, t)
        share = 1.0 / (counted[at, :] + counts)
        new = ((total[at, :] + sums) * share[:, 0:1]).astype(BF16)
        fresh_ref[0, at, :] = new
        new_f = new.astype(F32)
        square = jnp.sum(new_f * new_f, axis=1, keepdims=True)
        square = jnp.broadcast_to(square, (tile, 128)).T[0:1]
        twice = (new_f * -2.0).astype(BF16)
        for i in range(cuts):
            spot = pl.ds(i * chunk, chunk)
            cross = lax.dot_general(
                rows[i].reshape(chunk, feats), twice, (((1,), (1,)), ((), ())),
                preferred_element_type=F32,
            )
            near_sq = square + cross
            low = lowest[spot, :]
            for k in range(0, tile, 128):
                low = jnp.minimum(low, near_sq[:, k:k + 128])
            lowest[spot, :] = low
        return carry

    lax.fori_loop(0, tiles, finish, 0)
    for i in range(cuts):
        for j in range(groups):
            spot = pl.ds((i * groups + j) * lanes, lanes)
            low_out[j, i:i + 1, :] = jnp.min(lowest[spot, :].T, axis=0, keepdims=True)
    each_other(lambda flat: low_copy(flat).start())
    low_in[me] = low_out[g]

    for i in range(cuts):
        for s in order:
            z_copy(lax.rem(g + s, groups), i).wait_send()
        for j in sources:
            for s in range(1, xs):
                x_copy(j, s, i).wait_send()
                core_copy(j, lax.rem(x + s, xs) * 2 + core, i).wait_send()
            core_copy(j, m, i).wait_send()
    each_other(low_arrival)
    best = jnp.zeros((1, tok), F32)
    for c in range(groups):
        least = low_in[c * mems]
        for mm in range(1, mems):
            least = jnp.minimum(least, low_in[c * mems + mm])
        for i in range(cuts):
            column = jnp.broadcast_to(least[i:i + 1], (128, lanes)).T[:, 0:1]
            best += jnp.sum(jnp.where(spread(c, i), column, 0.0), axis=0, keepdims=True)
    cost_ref[...] = (row_sq + best) / feats


def local(points, cluster, assign, centroids, prior_counts):
    groups = lax.axis_size("grp")
    mems = lax.axis_size("mem")
    tok, feats = points.shape
    width = centroids.shape[1]
    cut = 128 // mems
    cap = round_up(2 * tok // groups, cut)
    cuts = cap // cut
    everyone = groups * mems
    xs = mems // 2
    dma = pltpu.SemaphoreType.DMA
    vmem = pl.BlockSpec(memory_space=pltpu.VMEM)
    anywhere = pl.BlockSpec(memory_space=pl.ANY)
    fresh, cost = pl.pallas_call(
        functools.partial(kernel, groups, mems, cut),
        out_shape=(
            pltpu.VMEM(centroids.shape, BF16),
            jax.ShapeDtypeStruct((1, tok), F32),
        ),
        in_specs=[vmem, vmem, vmem, vmem, anywhere],
        out_specs=(vmem, vmem),
        scratch_shapes=[
            pltpu.VMEM((groups, cap, feats), BF16),
            pltpu.VMEM((cuts, groups, mems, cut, feats), BF16),
            pltpu.VMEM((groups, 8, 128), jnp.int32),
            pltpu.VMEM((everyone, 8, 128), jnp.int32),
            pltpu.VMEM((groups, 8, 128), F32),
            pltpu.VMEM((everyone, 8, 128), F32),
            pltpu.VMEM((width, feats), BF16),
            pltpu.VMEM((width, feats), F32),
            pltpu.VMEM((width, 128), F32),
            pltpu.VMEM((everyone * cap, 128), F32),
            dma((groups, cuts)),
            dma((groups, max(1, xs - 1), cuts)),
            dma((groups, mems, cuts)),
            dma((groups, mems, cuts)),
            dma((everyone,)),
            dma((everyone,)),
            dma((everyone,)),
            dma((everyone,)),
            dma,
        ],
        compiler_params=pltpu.CompilerParams(
            collective_id=0, has_side_effects=True, vmem_limit_bytes=48 * 1024 * 1024
        ),
        cost_estimate=pl.CostEstimate(
            flops=4 * everyone * cap * width * feats,
            bytes_accessed=4 * width * feats + 2 * tok * feats,
            transcendentals=0,
        ),
    )(points, cluster.reshape(1, tok), assign.reshape(1, tok), prior_counts, centroids)
    return fresh, cost.reshape(tok)


def solution(mesh):
    placed = (
        P(("parts", "grp", "mem"), None),
        P(("parts", "grp", "mem"), None),
        P(("parts", "grp", "mem")),
        P(("parts", "grp"), "mem", None),
        P(("parts", "grp"), "mem"),
    )
    return jax.shard_map(
        local,
        mesh=mesh,
        in_specs=placed,
        out_specs=(P(("parts", "grp"), "mem", None), P(("parts", "grp", "mem"))),
        check_vma=False,
    )
```

```python
import functools

import jax
import jax.numpy as jnp
from jax import lax
from jax.experimental import pallas as pl
from jax.experimental.pallas import tpu as pltpu
from jax.sharding import PartitionSpec as P

MESH = pl.DeviceIdType.MESH
F32 = jnp.float32
BF16 = jnp.bfloat16
LAG = 3


def round_up(value, unit):
    return (value + unit - 1) // unit * unit


def kernel(
    groups, mems, cut, points_ref, cluster_ref, assign_ref, prior_ref, old_ref,
    fresh_ref, cost_ref,
    send_rows, rows, ids_out, ids_in, low_out, low_in, old, total, counted, low_row,
    z_send, x_send, core_send, row_recv, ids_send, ids_recv, low_send, low_recv, old_sem,
):
    tok, feats = points_ref.shape
    width = old.shape[0]
    everyone = groups * mems
    xs = mems // 2
    cuts = rows.shape[0]
    cap = cuts * cut
    lanes = mems * cut
    tile = min(256, width)
    tiles = width // tile
    g = lax.axis_index("grp")
    m = lax.axis_index("mem")
    x = m // 2
    core = m % 2
    near = m + 1 - 2 * core
    me = g * mems + m

    load_old = pltpu.make_async_copy(old_ref.at[0], old, old_sem)
    load_old.start()

    def where_is(flat):
        return {"grp": flat // mems, "mem": flat % mems}

    def each_other(body):
        def one(step, carry):
            body(lax.rem(me + step, everyone))
            return carry

        lax.fori_loop(1, everyone, one, 0, unroll=everyone <= 16)

    barrier = pltpu.get_barrier_semaphore()
    each_other(
        lambda flat: pl.semaphore_signal(
            barrier, inc=1, device_id=where_is(flat), device_id_type=MESH
        )
    )

    member = cluster_ref[...] == lax.broadcasted_iota(jnp.int32, (groups, tok), 0)
    before = lax.broadcasted_iota(jnp.int32, (tok, tok), 0) < lax.broadcasted_iota(
        jnp.int32, (tok, tok), 1
    )
    rank = jnp.dot(
        member.astype(F32).astype(BF16), before.astype(F32).astype(BF16),
        preferred_element_type=F32,
    )
    first_slot = (lax.broadcasted_iota(jnp.int32, (groups, tok), 0) * cap).astype(F32)
    target = jnp.sum(jnp.where(member, rank + first_slot, 0.0), axis=0, keepdims=True).astype(
        jnp.int32
    )

    points = points_ref[...]
    for c in range(groups):
        slot = lax.broadcasted_iota(jnp.int32, (cap, tok), 0) + c * cap
        place = (slot == target).astype(F32).astype(BF16)
        send_rows[c] = jnp.dot(place, points, preferred_element_type=F32).astype(BF16)

    lane = lax.broadcasted_iota(jnp.int32, (lanes, tok), 0) - m * cut
    own_lane = jnp.where((lane >= 0) & (lane < cut), lane, -groups * cap)

    def spread(c, i):
        return own_lane + (c * cap + i * cut) == target

    pl.semaphore_wait(barrier, everyone - 1)

    def copy(src, dst, send, recv, where):
        return pltpu.make_async_remote_copy(
            src_ref=src, dst_ref=dst, send_sem=send, recv_sem=recv, device_id=where,
            device_id_type=MESH,
        )

    def z_copy(c, i):
        return copy(
            send_rows.at[c, pl.ds(i * cut, cut)], rows.at[i, g, m], z_send.at[c, i],
            row_recv.at[g, m, i], {"grp": c},
        )

    def x_copy(j, s, i):
        there = lax.rem(x + s, xs) * 2 + core
        spot = rows.at[i, j, m]
        return copy(spot, spot, x_send.at[j, s - 1, i], row_recv.at[j, m, i], {"mem": there})

    def core_copy(j, mm, i):
        spot = rows.at[i, j, mm]
        return copy(spot, spot, core_send.at[j, mm, i], row_recv.at[j, mm, i], {"mem": near})

    def wait_rows(j, mm, i):
        core_copy(j, mm, i).wait_recv()

    def ids_copy(flat):
        return copy(
            ids_out.at[flat // mems], ids_in.at[me], ids_send.at[flat], ids_recv.at[me],
            where_is(flat),
        )

    def ids_arrival(flat):
        copy(
            ids_out.at[flat // mems], ids_in.at[flat], ids_send.at[flat], ids_recv.at[flat],
            where_is(flat),
        ).wait()

    def low_copy(flat):
        return copy(
            low_out.at[flat // mems], low_in.at[me], low_send.at[flat], low_recv.at[me],
            where_is(flat),
        )

    def low_arrival(flat):
        copy(
            low_out.at[flat // mems], low_in.at[flat], low_send.at[flat], low_recv.at[flat],
            where_is(flat),
        ).wait()

    half = groups // 2
    order = [half] + [s for d in range(1, half) for s in (half - d, half + d)]
    for i in range(cuts):
        for s in order:
            z_copy(lax.rem(g + s, groups), i).start()

    def forward_own(j, i):
        for s in range(1, xs):
            x_copy(j, s, i).start()
        core_copy(j, m, i).start()

    for i in range(cuts):
        rows[i, g, m] = send_rows[g, i * cut:(i + 1) * cut]
    for i in range(cuts):
        forward_own(g, i)

    assign = assign_ref[...]
    digit = lax.broadcasted_iota(jnp.int32, (8, tok), 0)
    digits = jnp.where(
        digit == 0, assign // 256, jnp.where(digit == 1, assign % 256, 1)
    ).astype(F32).astype(BF16)
    for c in range(groups):
        for i in range(cuts):
            found = lax.dot_general(
                digits, spread(c, i).astype(F32).astype(BF16), (((1,), (1,)), ((), ())),
                preferred_element_type=F32,
            ).astype(jnp.int32)
            ids_out[c, i:i + 1, :] = jnp.where(
                found[2:3] > 0, found[0:1] * 256 + found[1:2], -1
            )
    each_other(lambda flat: ids_copy(flat).start())
    ids_in[me] = ids_out[g]

    counted[...] = jnp.broadcast_to(prior_ref[...].astype(F32), (128, width)).T
    load_old.wait()

    def weigh(t, carry):
        at = pl.ds(pl.multiple_of(t * tile, tile), tile)
        total[at, :] = old[at, :].astype(F32) * counted[at, 0:1]
        return carry

    lax.fori_loop(0, tiles, weigh, 0)
    values = points.astype(F32)
    row_sq = jnp.sum(values * values, axis=1, keepdims=True)
    row_sq = jnp.broadcast_to(row_sq, (tok, 128)).T[0:1]

    chunk = groups * lanes
    first_code = m * width
    ones = jnp.ones((chunk, 128), BF16)

    def chunk_codes(i):
        found = []
        for j in range(groups):
            codes = ids_in[j * mems, i:i + 1, :]
            for mm in range(1, mems):
                codes = jnp.maximum(codes, ids_in[j * mems + mm, i:i + 1, :])
            found.append(codes)
        return jnp.concatenate(found, axis=1)

    def summed(codes, i, t):
        code = lax.broadcasted_iota(jnp.int32, (tile, chunk), 0) + (first_code + t * tile)
        onehot = (code == codes).astype(F32).astype(BF16)
        sums = jnp.dot(onehot, rows[i].reshape(chunk, feats), preferred_element_type=F32)
        return sums, jnp.dot(onehot, ones, preferred_element_type=F32)

    def add_chunk(i):
        codes = chunk_codes(i)

        def one(t, carry):
            at = pl.ds(pl.multiple_of(t * tile, tile), tile)
            sums, counts = summed(codes, i, t)
            total[at, :] += sums
            counted[at, :] += counts
            return carry

        lax.fori_loop(0, tiles, one, 0)

    def x_arrivals(j, i):
        for s in range(1, xs):
            mm = lax.rem(x + s, xs) * 2 + core
            wait_rows(j, mm, i)
            core_copy(j, mm, i).start()

    def core_arrivals(i):
        for j in sources:
            for s in range(xs):
                wait_rows(j, lax.rem(x + s, xs) * 2 + 1 - core, i)

    sources = [g] + [lax.rem(g + groups - s, groups) for s in order]
    ticks = [(i, step) for i in range(cuts) for step in range(1, groups)]
    queue = [(i, 0) for i in range(cuts)] + ticks
    done = 0
    for n, (i, step) in enumerate(ticks):
        wait_rows(sources[step], m, i)
        forward_own(sources[step], i)
        while done <= n + cuts - LAG:
            x_arrivals(sources[queue[done][1]], queue[done][0])
            done += 1
    added = 0
    each_other(ids_arrival)
    while done < len(queue):
        x_arrivals(sources[queue[done][1]], queue[done][0])
        done += 1
        if done >= cuts + (added + 1) * (groups - 1) + 1 and added < cuts - 1:
            core_arrivals(added)
            add_chunk(added)
            added += 1
    while added < cuts - 1:
        core_arrivals(added)
        add_chunk(added)
        added += 1
    core_arrivals(cuts - 1)

    codes = chunk_codes(cuts - 1)
    low_row[...] = jnp.full(low_row.shape, jnp.inf, F32)

    def finish(t, carry):
        at = pl.ds(pl.multiple_of(t * tile, tile), tile)
        sums, counts = summed(codes, cuts - 1, t)
        share = 1.0 / (counted[at, :] + counts)
        new = ((total[at, :] + sums) * share[:, 0:1]).astype(BF16)
        fresh_ref[0, at, :] = new
        new_f = new.astype(F32)
        square = jnp.sum(new_f * new_f, axis=1, keepdims=True)
        twice = (new_f * -2.0).astype(BF16)
        for i in range(cuts):
            cross = lax.dot_general(
                twice, rows[i].reshape(chunk, feats), (((1,), (1,)), ((), ())),
                preferred_element_type=F32,
            )
            low_row[i:i + 1, :] = jnp.minimum(low_row[i:i + 1, :], jnp.min(square + cross, axis=0, keepdims=True))
        return carry

    lax.fori_loop(0, tiles, finish, 0)
    for i in range(cuts):
        for j in range(groups):
            low_out[j, i:i + 1, :] = low_row[i:i + 1, j * lanes:(j + 1) * lanes]
    each_other(lambda flat: low_copy(flat).start())
    low_in[me] = low_out[g]

    for i in range(cuts):
        for s in order:
            z_copy(lax.rem(g + s, groups), i).wait_send()
        for j in sources:
            for s in range(1, xs):
                x_copy(j, s, i).wait_send()
                core_copy(j, lax.rem(x + s, xs) * 2 + core, i).wait_send()
            core_copy(j, m, i).wait_send()
    each_other(low_arrival)
    best = jnp.zeros((1, tok), F32)
    for c in range(groups):
        least = low_in[c * mems]
        for mm in range(1, mems):
            least = jnp.minimum(least, low_in[c * mems + mm])
        for i in range(cuts):
            column = jnp.broadcast_to(least[i:i + 1], (128, lanes)).T[:, 0:1]
            best += jnp.sum(jnp.where(spread(c, i), column, 0.0), axis=0, keepdims=True)
    cost_ref[...] = (row_sq + best) / feats


def local(points, cluster, assign, centroids, prior_counts):
    groups = lax.axis_size("grp")
    mems = lax.axis_size("mem")
    tok, feats = points.shape
    width = centroids.shape[1]
    cut = 128 // mems
    cap = round_up(2 * tok // groups, cut)
    cuts = cap // cut
    everyone = groups * mems
    xs = mems // 2
    dma = pltpu.SemaphoreType.DMA
    vmem = pl.BlockSpec(memory_space=pltpu.VMEM)
    anywhere = pl.BlockSpec(memory_space=pl.ANY)
    fresh, cost = pl.pallas_call(
        functools.partial(kernel, groups, mems, cut),
        out_shape=(
            pltpu.VMEM(centroids.shape, BF16),
            jax.ShapeDtypeStruct((1, tok), F32),
        ),
        in_specs=[vmem, vmem, vmem, vmem, anywhere],
        out_specs=(vmem, vmem),
        scratch_shapes=[
            pltpu.VMEM((groups, cap, feats), BF16),
            pltpu.VMEM((cuts, groups, mems, cut, feats), BF16),
            pltpu.VMEM((groups, 8, 128), jnp.int32),
            pltpu.VMEM((everyone, 8, 128), jnp.int32),
            pltpu.VMEM((groups, 8, 128), F32),
            pltpu.VMEM((everyone, 8, 128), F32),
            pltpu.VMEM((width, feats), BF16),
            pltpu.VMEM((width, feats), F32),
            pltpu.VMEM((width, 128), F32),
            pltpu.VMEM((round_up(cuts, 8), groups * 128), F32),
            dma((groups, cuts)),
            dma((groups, max(1, xs - 1), cuts)),
            dma((groups, mems, cuts)),
            dma((groups, mems, cuts)),
            dma((everyone,)),
            dma((everyone,)),
            dma((everyone,)),
            dma((everyone,)),
            dma,
        ],
        compiler_params=pltpu.CompilerParams(
            collective_id=0, has_side_effects=True, vmem_limit_bytes=48 * 1024 * 1024
        ),
        cost_estimate=pl.CostEstimate(
            flops=4 * everyone * cap * width * feats,
            bytes_accessed=4 * width * feats + 2 * tok * feats,
            transcendentals=0,
        ),
    )(points, cluster.reshape(1, tok), assign.reshape(1, tok), prior_counts, centroids)
    return fresh, cost.reshape(tok)


def solution(mesh):
    placed = (
        P(("parts", "grp", "mem"), None),
        P(("parts", "grp", "mem"), None),
        P(("parts", "grp", "mem")),
        P(("parts", "grp"), "mem", None),
        P(("parts", "grp"), "mem"),
    )
    return jax.shard_map(
        local,
        mesh=mesh,
        in_specs=placed,
        out_specs=(P(("parts", "grp"), "mem", None), P(("parts", "grp", "mem"))),
        check_vma=False,
    )
```

```python
import functools

import jax
import jax.numpy as jnp
from jax import lax
from jax.experimental import pallas as pl
from jax.experimental.pallas import tpu as pltpu
from jax.sharding import PartitionSpec as P

MESH = pl.DeviceIdType.MESH
F32 = jnp.float32
BF16 = jnp.bfloat16
LAG = 3


def round_up(value, unit):
    return (value + unit - 1) // unit * unit


def kernel(
    groups, mems, cut, points_ref, cluster_ref, assign_ref, prior_ref, old_ref,
    fresh_ref, cost_ref,
    send_rows, rows, ids_out, ids_in, low_out, low_in, old, total, counted, low_row,
    z_send, x_send, core_send, row_recv, ids_send, ids_recv, low_send, low_recv, old_sem,
):
    tok, feats = points_ref.shape
    width = old.shape[0]
    everyone = groups * mems
    xs = mems // 2
    cuts = rows.shape[0]
    cap = cuts * cut
    lanes = mems * cut
    tile = min(256, width)
    tiles = width // tile
    g = lax.axis_index("grp")
    m = lax.axis_index("mem")
    x = m // 2
    core = m % 2
    near = m + 1 - 2 * core
    me = g * mems + m

    load_old = pltpu.make_async_copy(old_ref.at[0], old, old_sem)
    load_old.start()

    def where_is(flat):
        return {"grp": flat // mems, "mem": flat % mems}

    def each_other(body):
        def one(step, carry):
            body(lax.rem(me + step, everyone))
            return carry

        lax.fori_loop(1, everyone, one, 0, unroll=everyone <= 16)

    barrier = pltpu.get_barrier_semaphore()
    each_other(
        lambda flat: pl.semaphore_signal(
            barrier, inc=1, device_id=where_is(flat), device_id_type=MESH
        )
    )

    member = cluster_ref[...] == lax.broadcasted_iota(jnp.int32, (groups, tok), 0)
    before = lax.broadcasted_iota(jnp.int32, (tok, tok), 0) < lax.broadcasted_iota(
        jnp.int32, (tok, tok), 1
    )
    rank = jnp.dot(
        member.astype(F32).astype(BF16), before.astype(F32).astype(BF16),
        preferred_element_type=F32,
    )
    first_slot = (lax.broadcasted_iota(jnp.int32, (groups, tok), 0) * cap).astype(F32)
    target = jnp.sum(jnp.where(member, rank + first_slot, 0.0), axis=0, keepdims=True).astype(
        jnp.int32
    )

    points = points_ref[...]
    for c in range(groups):
        slot = lax.broadcasted_iota(jnp.int32, (cap, tok), 0) + c * cap
        place = (slot == target).astype(F32).astype(BF16)
        send_rows[c] = jnp.dot(place, points, preferred_element_type=F32).astype(BF16)

    lane = lax.broadcasted_iota(jnp.int32, (lanes, tok), 0) - m * cut
    own_lane = jnp.where((lane >= 0) & (lane < cut), lane, -groups * cap)

    def spread(c, i):
        return own_lane + (c * cap + i * cut) == target

    pl.semaphore_wait(barrier, everyone - 1)

    def copy(src, dst, send, recv, where):
        return pltpu.make_async_remote_copy(
            src_ref=src, dst_ref=dst, send_sem=send, recv_sem=recv, device_id=where,
            device_id_type=MESH,
        )

    def z_copy(c, i):
        return copy(
            send_rows.at[c, pl.ds(i * cut, cut)], rows.at[i, g, m], z_send.at[c, i],
            row_recv.at[g, m, i], {"grp": c},
        )

    def x_copy(j, s, i):
        there = lax.rem(x + s, xs) * 2 + core
        spot = rows.at[i, j, m]
        return copy(spot, spot, x_send.at[j, s - 1, i], row_recv.at[j, m, i], {"mem": there})

    def core_copy(j, mm, i):
        spot = rows.at[i, j, mm]
        return copy(spot, spot, core_send.at[j, mm, i], row_recv.at[j, mm, i], {"mem": near})

    def wait_rows(j, mm, i):
        core_copy(j, mm, i).wait_recv()

    def ids_copy(flat):
        return copy(
            ids_out.at[flat // mems], ids_in.at[me], ids_send.at[flat], ids_recv.at[me],
            where_is(flat),
        )

    def ids_arrival(flat):
        copy(
            ids_out.at[flat // mems], ids_in.at[flat], ids_send.at[flat], ids_recv.at[flat],
            where_is(flat),
        ).wait()

    def low_copy(flat):
        return copy(
            low_out.at[flat // mems], low_in.at[me], low_send.at[flat], low_recv.at[me],
            where_is(flat),
        )

    def low_arrival(flat):
        copy(
            low_out.at[flat // mems], low_in.at[flat], low_send.at[flat], low_recv.at[flat],
            where_is(flat),
        ).wait()

    half = groups // 2

    def far(k):
        up = jnp.where(groups - k > g, groups - k, groups - 1 - k)
        down = jnp.where(k - 1 < g, k - 1, k)
        return jnp.where(g < half, up, down)

    order = [half] + [s for d in range(1, half) for s in (half - d, half + d)]

    def forward_own(j, i):
        for s in range(1, xs):
            x_copy(j, s, i).start()
        core_copy(j, m, i).start()

    for i in range(cuts):
        rows[i, g, m] = send_rows[g, i * cut:(i + 1) * cut]
    for i in range(cuts):
        for s in range(1, groups):
            z_copy(far(s), i).start()
        forward_own(g, i)

    assign = assign_ref[...]
    digit = lax.broadcasted_iota(jnp.int32, (8, tok), 0)
    digits = jnp.where(
        digit == 0, assign // 256, jnp.where(digit == 1, assign % 256, 1)
    ).astype(F32).astype(BF16)
    for c in range(groups):
        for i in range(cuts):
            found = lax.dot_general(
                digits, spread(c, i).astype(F32).astype(BF16), (((1,), (1,)), ((), ())),
                preferred_element_type=F32,
            ).astype(jnp.int32)
            ids_out[c, i:i + 1, :] = jnp.where(
                found[2:3] > 0, found[0:1] * 256 + found[1:2], -1
            )
    each_other(lambda flat: ids_copy(flat).start())
    ids_in[me] = ids_out[g]

    counted[...] = jnp.broadcast_to(prior_ref[...].astype(F32), (128, width)).T
    load_old.wait()

    def weigh(t, carry):
        at = pl.ds(pl.multiple_of(t * tile, tile), tile)
        total[at, :] = old[at, :].astype(F32) * counted[at, 0:1]
        return carry

    lax.fori_loop(0, tiles, weigh, 0)
    values = points.astype(F32)
    row_sq = jnp.sum(values * values, axis=1, keepdims=True)
    row_sq = jnp.broadcast_to(row_sq, (tok, 128)).T[0:1]

    chunk = groups * lanes
    first_code = m * width
    ones = jnp.ones((chunk, 128), BF16)

    def chunk_codes(i):
        found = []
        for j in range(groups):
            codes = ids_in[j * mems, i:i + 1, :]
            for mm in range(1, mems):
                codes = jnp.maximum(codes, ids_in[j * mems + mm, i:i + 1, :])
            found.append(codes)
        return jnp.concatenate(found, axis=1)

    def summed(codes, i, t):
        code = lax.broadcasted_iota(jnp.int32, (tile, chunk), 0) + (first_code + t * tile)
        onehot = (code == codes).astype(F32).astype(BF16)
        sums = jnp.dot(onehot, rows[i].reshape(chunk, feats), preferred_element_type=F32)
        return sums, jnp.dot(onehot, ones, preferred_element_type=F32)

    def add_chunk(i):
        codes = chunk_codes(i)

        def one(t, carry):
            at = pl.ds(pl.multiple_of(t * tile, tile), tile)
            sums, counts = summed(codes, i, t)
            total[at, :] += sums
            counted[at, :] += counts
            return carry

        lax.fori_loop(0, tiles, one, 0)

    def x_arrivals(j, i):
        for s in range(1, xs):
            mm = lax.rem(x + s, xs) * 2 + core
            wait_rows(j, mm, i)
            core_copy(j, mm, i).start()

    def core_arrivals(i):
        for j in sources:
            for s in range(xs):
                wait_rows(j, lax.rem(x + s, xs) * 2 + 1 - core, i)

    sources = [g] + [far(s) for s in range(1, groups)]
    ticks = [(i, step) for i in range(cuts) for step in range(1, groups)]
    queue = [(i, 0) for i in range(cuts)] + ticks
    done = 0
    for n, (i, step) in enumerate(ticks):
        wait_rows(sources[step], m, i)
        forward_own(sources[step], i)
        while done <= n + cuts - LAG:
            x_arrivals(sources[queue[done][1]], queue[done][0])
            done += 1
    added = 0
    each_other(ids_arrival)
    while done < len(queue):
        x_arrivals(sources[queue[done][1]], queue[done][0])
        done += 1
        if done >= cuts + (added + 1) * (groups - 1) + 1 and added < cuts - 1:
            core_arrivals(added)
            add_chunk(added)
            added += 1
    while added < cuts - 1:
        core_arrivals(added)
        add_chunk(added)
        added += 1
    core_arrivals(cuts - 1)

    codes = chunk_codes(cuts - 1)
    low_row[...] = jnp.full(low_row.shape, jnp.inf, F32)

    def finish(t, carry):
        at = pl.ds(pl.multiple_of(t * tile, tile), tile)
        sums, counts = summed(codes, cuts - 1, t)
        share = 1.0 / (counted[at, :] + counts)
        new = ((total[at, :] + sums) * share[:, 0:1]).astype(BF16)
        fresh_ref[0, at, :] = new
        new_f = new.astype(F32)
        square = jnp.sum(new_f * new_f, axis=1, keepdims=True)
        twice = (new_f * -2.0).astype(BF16)
        for i in range(cuts):
            cross = lax.dot_general(
                twice, rows[i].reshape(chunk, feats), (((1,), (1,)), ((), ())),
                preferred_element_type=F32,
            )
            low_row[i:i + 1, :] = jnp.minimum(low_row[i:i + 1, :], jnp.min(square + cross, axis=0, keepdims=True))
        return carry

    lax.fori_loop(0, tiles, finish, 0)
    for i in range(cuts):
        for j in range(groups):
            low_out[j, i:i + 1, :] = low_row[i:i + 1, j * lanes:(j + 1) * lanes]
    each_other(lambda flat: low_copy(flat).start())
    low_in[me] = low_out[g]

    for i in range(cuts):
        for s in order:
            z_copy(lax.rem(g + s, groups), i).wait_send()
        for j in sources:
            for s in range(1, xs):
                x_copy(j, s, i).wait_send()
                core_copy(j, lax.rem(x + s, xs) * 2 + core, i).wait_send()
            core_copy(j, m, i).wait_send()
    each_other(low_arrival)
    best = jnp.zeros((1, tok), F32)
    for c in range(groups):
        least = low_in[c * mems]
        for mm in range(1, mems):
            least = jnp.minimum(least, low_in[c * mems + mm])
        for i in range(cuts):
            column = jnp.broadcast_to(least[i:i + 1], (128, lanes)).T[:, 0:1]
            best += jnp.sum(jnp.where(spread(c, i), column, 0.0), axis=0, keepdims=True)
    cost_ref[...] = (row_sq + best) / feats


def local(points, cluster, assign, centroids, prior_counts):
    groups = lax.axis_size("grp")
    mems = lax.axis_size("mem")
    tok, feats = points.shape
    width = centroids.shape[1]
    cut = 128 // mems
    cap = round_up(2 * tok // groups, cut)
    cuts = cap // cut
    everyone = groups * mems
    xs = mems // 2
    dma = pltpu.SemaphoreType.DMA
    vmem = pl.BlockSpec(memory_space=pltpu.VMEM)
    anywhere = pl.BlockSpec(memory_space=pl.ANY)
    fresh, cost = pl.pallas_call(
        functools.partial(kernel, groups, mems, cut),
        out_shape=(
            pltpu.VMEM(centroids.shape, BF16),
            jax.ShapeDtypeStruct((1, tok), F32),
        ),
        in_specs=[vmem, vmem, vmem, vmem, anywhere],
        out_specs=(vmem, vmem),
        scratch_shapes=[
            pltpu.VMEM((groups, cap, feats), BF16),
            pltpu.VMEM((cuts, groups, mems, cut, feats), BF16),
            pltpu.VMEM((groups, 8, 128), jnp.int32),
            pltpu.VMEM((everyone, 8, 128), jnp.int32),
            pltpu.VMEM((groups, 8, 128), F32),
            pltpu.VMEM((everyone, 8, 128), F32),
            pltpu.VMEM((width, feats), BF16),
            pltpu.VMEM((width, feats), F32),
            pltpu.VMEM((width, 128), F32),
            pltpu.VMEM((round_up(cuts, 8), groups * 128), F32),
            dma((groups, cuts)),
            dma((groups, max(1, xs - 1), cuts)),
            dma((groups, mems, cuts)),
            dma((groups, mems, cuts)),
            dma((everyone,)),
            dma((everyone,)),
            dma((everyone,)),
            dma((everyone,)),
            dma,
        ],
        compiler_params=pltpu.CompilerParams(
            collective_id=0, has_side_effects=True, vmem_limit_bytes=48 * 1024 * 1024
        ),
        cost_estimate=pl.CostEstimate(
            flops=4 * everyone * cap * width * feats,
            bytes_accessed=4 * width * feats + 2 * tok * feats,
            transcendentals=0,
        ),
    )(points, cluster.reshape(1, tok), assign.reshape(1, tok), prior_counts, centroids)
    return fresh, cost.reshape(tok)


def solution(mesh):
    placed = (
        P(("parts", "grp", "mem"), None),
        P(("parts", "grp", "mem"), None),
        P(("parts", "grp", "mem")),
        P(("parts", "grp"), "mem", None),
        P(("parts", "grp"), "mem"),
    )
    return jax.shard_map(
        local,
        mesh=mesh,
        in_specs=placed,
        out_specs=(P(("parts", "grp"), "mem", None), P(("parts", "grp", "mem"))),
        check_vma=False,
    )
```
